32 devices in a mesh: dp: 2 (over x), outer: 8 (over z, y), inner: 2 (over core).
Axes of the slice: x: 2, y: 2, z: 4, core: 2. Of those that a mesh axis runs over, the one named last changes fastest.
Arguments:
- tokens: bfloat16 [1024, 4096], P(('dp', 'outer', 'inner')), may hold values from -6 to 6
- expert_ids: int32 [1024, 8], P(('dp', 'outer', 'inner')), may hold values from 0 to 15, all different within a row; in each aligned block of 32 rows (0 to 31, 32 to 63, ...) at most 24 rows name the same one
- gate_values: float32 [1024, 8], P(('dp', 'outer', 'inner')), may hold values from 0.02 to 0.5
- upstream: bfloat16 [1024, 4096], P(('dp', 'outer', 'inner')), may hold values from -1.5 to 1.5
- w_gate: bfloat16 [16, 4096, 768], P(('outer', 'inner')), may hold values from -0.09375 to 0.09375
- w_up: bfloat16 [16, 4096, 768], P(('outer', 'inner')), may hold values from -0.09375 to 0.09375
- w_down: bfloat16 [16, 768, 4096], P(('outer', 'inner')), may hold values from -0.21875 to 0.21875
Outputs:
- output: bfloat16 [1024, 4096], P(('dp', 'outer', 'inner'))
- grad_tokens: bfloat16 [1024, 4096], P(('dp', 'outer', 'inner'))
- grad_gates: float32 [1024, 8], P(('dp', 'outer', 'inner'))
- grad_w_gate: bfloat16 [16, 4096, 768], P(('outer', 'inner'), 'dp')
- grad_w_up: bfloat16 [16, 4096, 768], P(('outer', 'inner'), 'dp')
- grad_w_down: bfloat16 [16, 768, 4096], P(('outer', 'inner'), None, 'dp')
The draws below stay inside these ranges and needn't reach their ends.
Inputs may be any that keep to these rules, and one draw needn't show every extreme that they name: `expert_ids`: each token names 8 different experts. Among the 32 tokens of one device (aligned blocks of rows), no expert is named more than 24 times, a bound that some block reaches.
All inputs are finite; a program needn't handle non-finite values.
Results may differ from the reference program's by a relative error of at most 0.013.
Values may be sent and summed in bfloat16 or wider, within the bound.
A program may use at most 192 MiB of HBM per device.

```python
import math
import jax
import jax.numpy as jnp
import numpy as np
from jax import lax

D = 4096
TOP = 8
FF = 768
TOK_DEV = 32
EXPERTS = 16
TOKENS = 1024
CAP = 24
N_DP = 2


def shard_levels(stream_key, dims, cuts, smallest, high):
    gain = 1.0
    for axis_at, blocks in cuts:
        draws = jax.random.uniform(jax.random.fold_in(jax.random.fold_in(stream_key, 6), axis_at), (blocks,), jnp.float32, smallest / len(cuts), high / len(cuts))
        gain = gain * jnp.repeat(jnp.exp(draws), dims[axis_at] // blocks).reshape((-1,) + (1,) * (len(dims) - 1 - axis_at))
    return gain


def deal_out(key, own, number, rows, number_of, top, reach, skew):
    order = jax.random.permutation(key, number_of)
    packed, usual = portions_of(number_of, rows * top, reach, skew, True), portions_of(number_of, rows * top, reach, skew, False)
    places = jnp.arange(number_of)

    def named(sizes, turn):
        used = int((sizes > 0).sum())
        fixed = max(1, used // 4)
        moved = fixed + (places - fixed + turn * (used - fixed)) % max(1, number_of - fixed)
        return jnp.zeros((number_of,), jnp.int32).at[order[jnp.where(places < fixed, places, moved)]].set(jnp.asarray(sizes, jnp.int32))

    sizes = jnp.where(number % 4 == 0, named(packed, number // 4), named(usual, number - number // 4 - 1))
    mixed = jax.random.permutation(jax.random.fold_in(own, 3), number_of)
    source_of, receiver = mixed[0:number_of // 2 * 2:2], mixed[1:number_of // 2 * 2:2]
    room = jnp.minimum(sizes[source_of] - 1, reach - sizes[receiver]) // 2
    room = jnp.where((source_of == order[0]) | (receiver == order[0]) | (sizes[receiver] == 0), 0, jnp.maximum(room, 0))
    moved = jax.random.randint(jax.random.fold_in(own, 4), (number_of // 2,), 0, 1 << 20) % (room + 1)
    sizes = sizes.at[source_of].add(-moved).at[receiver].add(moved)
    items = jnp.searchsorted(jnp.cumsum(sizes), jnp.arange(rows * top), side="right").astype(jnp.int32)
    listing = items.reshape(top, rows).T
    listing = listing[jax.random.permutation(jax.random.fold_in(own, 1), rows)]
    turn = jax.random.randint(jax.random.fold_in(own, 2), (rows, 1), 0, top)
    return jnp.take_along_axis(listing, (jnp.arange(top)[None, :] + turn) % top, axis=1)


def portions_of(count, total, bound, skew, full):
    portions = [(1 << 20) // math.isqrt(grade ** skew) + 1 for grade in range(1, count + 1)]
    largest = bound if full else min(bound, max(-(-total // count), total * portions[0] // sum(portions)))
    least = 1 if total - largest >= count - 1 else 0
    given, surplus = [largest] + [least] * (count - 1), total - largest - least * (count - 1)
    while surplus > 0:
        candidates = [i for i in range(1, count) if given[i] < largest] or [i for i in range(1, count) if given[i] < bound]
        pool, budget = sum([portions[i] for i in candidates]), surplus
        for i in candidates:
            more = min(bound - given[i], max(1, budget * portions[i] // pool), surplus)
            given[i] = given[i] + more
            surplus = surplus - more
    return np.array(given)


def gaussian(own_key, dims, spread, most, pieces=(), held_as=jnp.bfloat16):
    values = jax.random.normal(own_key, dims, jnp.float32) * spread
    if len(pieces) > 0:
        values = shard_levels(own_key, dims, pieces, -0.22, 0.18) * values
    return jnp.clip(values, min=-most, max=most).astype(held_as)


def setup_inputs(seed: int = 0) -> dict:
    streams_of = jax.random.split(jax.random.key(seed), 8)
    tokens = gaussian(streams_of[0], (TOKENS, D), 1.0, 6.0, ((0, 32),))
    expert_ids_keys = jax.random.split(jax.random.fold_in(streams_of[1], 1), TOKENS // TOK_DEV)
    expert_ids_turns = jax.random.permutation(jax.random.fold_in(streams_of[1], 3), TOKENS // TOK_DEV)
    expert_ids = jax.vmap(lambda own, number: deal_out(jax.random.fold_in(streams_of[1], 2), own, number, TOK_DEV, EXPERTS, TOP, CAP, 1))(expert_ids_keys, expert_ids_turns).reshape((TOKENS, TOP))
    gate_values = jnp.clip(jnp.exp(math.log(0.5) - 3.218876 * jax.random.uniform(streams_of[2], (TOKENS, TOP), jnp.float32) ** shard_levels(streams_of[2], (TOKENS, TOP), ((0, 32),), -0.2, 0.2)), 0.02, 0.5)
    upstream = gaussian(streams_of[3], (TOKENS, D), 0.25, 1.5, ((0, 32),))
    w_gate = gaussian(streams_of[4], (EXPERTS, D, FF), D ** -0.5, 0.09375, ((0, 16),))
    w_up = gaussian(streams_of[5], (EXPERTS, D, FF), D ** -0.5, 0.09375, ((0, 16),))
    w_down = gaussian(streams_of[6], (EXPERTS, FF, D), FF ** -0.5, 0.21875, ((0, 16),))
    return dict(tokens=tokens, expert_ids=expert_ids, gate_values=gate_values, upstream=upstream, w_gate=w_gate, w_up=w_up, w_down=w_down)


block_rows = 64


def contract_last(left, right):
    return lax.dot_general(left, right, (((1,), (1,)), ((), ())), preferred_element_type=jnp.float32)


def contract_first(left, right):
    return lax.dot_general(left, right, (((0,), (0,)), ((), ())), preferred_element_type=jnp.float32)


def expert_rows(rows_in, grads_in, gate_mat, up_mat, down_mat):
    gate_pre = jnp.dot(rows_in, gate_mat, preferred_element_type=jnp.float32)
    up_pre = jnp.dot(rows_in, up_mat, preferred_element_type=jnp.float32)
    sigma = jax.nn.sigmoid(gate_pre)
    silu_value = gate_pre * sigma
    hidden = (silu_value * up_pre).astype(jnp.bfloat16)
    expert_out = jnp.dot(hidden, down_mat, preferred_element_type=jnp.float32).astype(jnp.bfloat16)
    grad_hidden = contract_last(grads_in, down_mat)
    slope = sigma * (1.0 + gate_pre * (1.0 - sigma))
    grad_gate_pre = (grad_hidden * up_pre * slope).astype(jnp.bfloat16)
    grad_up_pre = (grad_hidden * silu_value).astype(jnp.bfloat16)
    pair_grad = (contract_last(grad_gate_pre, gate_mat) + contract_last(grad_up_pre, up_mat)).astype(jnp.bfloat16)
    return hidden, expert_out, grad_gate_pre, grad_up_pre, pair_grad


def reference(tokens, expert_ids, gate_values, upstream, w_gate, w_up, w_down):
    group_tokens = TOKENS // N_DP
    group_pairs = group_tokens * TOP
    padded_rows = group_pairs + EXPERTS * block_rows
    block_count = padded_rows // block_rows
    total_gate = jnp.zeros((EXPERTS, D, FF), jnp.float32)
    total_up = jnp.zeros((EXPERTS, D, FF), jnp.float32)
    total_down = jnp.zeros((EXPERTS, FF, D), jnp.float32)
    out_list = []
    grad_list = []
    gate_grad_list = []
    for group in range(N_DP):
        first = group * group_tokens
        group_tok = tokens[first:first + group_tokens]
        group_up = upstream[first:first + group_tokens]
        flat_ids = expert_ids[first:first + group_tokens].reshape(-1)
        flat_gates = gate_values[first:first + group_tokens].reshape(-1)
        expert_iota = jnp.arange(EXPERTS, dtype=jnp.int32)
        counts = jnp.sum((flat_ids[:, None] == expert_iota[None, :]).astype(jnp.int32), axis=0)
        padded = (counts + block_rows - 1) // block_rows * block_rows
        pad_start = (jnp.cumsum(padded) - padded).astype(jnp.int32)
        plain_start = (jnp.cumsum(counts) - counts).astype(jnp.int32)
        order = jnp.argsort(flat_ids, stable=True).astype(jnp.int32)
        sorted_ids = flat_ids[order]
        position = (pad_start[sorted_ids] + jnp.arange(group_pairs, dtype=jnp.int32) - plain_start[sorted_ids]).astype(jnp.int32)
        slot_pair = jnp.full((padded_rows,), group_pairs, jnp.int32).at[position].set(order)
        pair_slot = jnp.zeros((group_pairs,), jnp.int32).at[order].set(position)
        block_first = jnp.arange(block_count, dtype=jnp.int32) * block_rows
        block_expert = jnp.clip(jnp.sum((pad_start[None, :] <= block_first[:, None]).astype(jnp.int32), axis=1) - 1, 0, EXPERTS - 1).astype(jnp.int32)
        pair_token = jnp.arange(group_pairs, dtype=jnp.int32) // TOP
        scaled = (flat_gates[:, None] * group_up[pair_token].astype(jnp.float32)).astype(jnp.bfloat16)
        token_pad = jnp.concatenate([group_tok, jnp.zeros((1, D), jnp.bfloat16)], axis=0)
        scaled_pad = jnp.concatenate([scaled, jnp.zeros((1, D), jnp.bfloat16)], axis=0)
        slot_token = jnp.where(slot_pair < group_pairs, slot_pair // TOP, group_tokens).astype(jnp.int32)

        def visit(carry, block_index):
            start = block_index * block_rows
            expert = block_expert[block_index]
            rows_in = token_pad[lax.dynamic_slice_in_dim(slot_token, start, block_rows)]
            grads_in = scaled_pad[lax.dynamic_slice_in_dim(slot_pair, start, block_rows)]
            hidden, expert_out, grad_gate_pre, grad_up_pre, pair_grad = expert_rows(
                rows_in, grads_in, w_gate[expert], w_up[expert], w_down[expert])
            part_gate, part_up, part_down = carry
            part_gate = part_gate.at[expert].add(contract_first(rows_in, grad_gate_pre))
            part_up = part_up.at[expert].add(contract_first(rows_in, grad_up_pre))
            part_down = part_down.at[expert].add(contract_first(hidden, grads_in))
            return (part_gate, part_up, part_down), (expert_out, pair_grad)

        start_parts = (jnp.zeros((EXPERTS, D, FF), jnp.float32), jnp.zeros((EXPERTS, D, FF), jnp.float32),
                       jnp.zeros((EXPERTS, FF, D), jnp.float32))
        parts, (block_out, block_grad) = lax.scan(visit, start_parts, jnp.arange(block_count, dtype=jnp.int32))
        total_gate = total_gate + lax.optimization_barrier(parts[0].astype(jnp.bfloat16)).astype(jnp.float32)
        total_up = total_up + lax.optimization_barrier(parts[1].astype(jnp.bfloat16)).astype(jnp.float32)
        total_down = total_down + lax.optimization_barrier(parts[2].astype(jnp.bfloat16)).astype(jnp.float32)
        pair_out = block_out.reshape(padded_rows, D)[pair_slot].reshape(group_tokens, TOP, D).astype(jnp.float32)
        pair_back = block_grad.reshape(padded_rows, D)[pair_slot].reshape(group_tokens, TOP, D).astype(jnp.float32)
        gates_grid = flat_gates.reshape(group_tokens, TOP)
        out_list.append(jnp.sum(gates_grid[:, :, None] * pair_out, axis=1).astype(jnp.bfloat16))
        grad_list.append(jnp.sum(pair_back, axis=1).astype(jnp.bfloat16))
        gate_grad_list.append(jnp.einsum("tkd,td->tk", pair_out, group_up.astype(jnp.float32)))
    output = jnp.concatenate(out_list, axis=0)
    grad_tokens = jnp.concatenate(grad_list, axis=0)
    grad_gates = jnp.concatenate(gate_grad_list, axis=0)
    return (output, grad_tokens, grad_gates, total_gate.astype(jnp.bfloat16),
            total_up.astype(jnp.bfloat16), total_down.astype(jnp.bfloat16))
```

```python
import jax
import jax.numpy as jnp
from jax import lax
from jax.sharding import PartitionSpec as P

PLANE = ("outer", "inner")


def dot(left, right, left_dim, right_dim):
    return lax.dot_general(
        left,
        right,
        (((left_dim,), (right_dim,)), ((), ())),
        preferred_element_type=jnp.float32,
    )


def exchange(block_for, count):
    me = lax.axis_index("dp")
    got = []
    for shift in range(1, count):
        pairs = [(q, (q + shift) % count) for q in range(count)]
        got.append(lax.ppermute(block_for((me + shift) % count), "dp", pairs))
    return got


def local(tokens, expert_ids, gate_values, upstream, w_gate, w_up, w_down):
    local_tokens, width = tokens.shape
    groups = lax.axis_size("dp")
    inner_count = lax.axis_size("inner")
    expert_count = lax.axis_size("outer") * inner_count
    me = lax.axis_index("dp")
    expert = lax.axis_index("outer") * inner_count + lax.axis_index("inner")
    share = width // groups
    gate_mat, up_mat, down_mat = w_gate[0], w_up[0], w_down[0]

    def plane_gather(value):
        return lax.all_gather(value, PLANE, axis=0, tiled=True)

    chosen = expert_ids[:, :, None] == jnp.arange(expert_count, dtype=jnp.int32)[None, None, :]
    gate_grid = jnp.sum(jnp.where(chosen, gate_values[:, :, None], 0.0), axis=1)

    all_tokens = plane_gather(tokens)
    all_gates = plane_gather(gate_grid)
    all_upstream = plane_gather(upstream)
    both = jnp.stack([tokens, upstream], axis=1)
    far = exchange(lambda j: lax.dynamic_slice_in_dim(both, j * share, share, 2), groups)
    far = [plane_gather(block) for block in far]

    is_mine = jnp.arange(expert_count, dtype=jnp.int32) == expert
    gate = jnp.sum(jnp.where(is_mine[None, :], all_gates, 0.0), axis=1, keepdims=True)

    gate_pre = dot(all_tokens, gate_mat, 1, 0)
    up_pre = dot(all_tokens, up_mat, 1, 0)
    grad_hidden = dot(all_upstream, down_mat, 1, 1)
    sigma = jax.nn.sigmoid(gate_pre)
    silu_value = gate_pre * sigma
    hidden = silu_value * up_pre
    slope = sigma * (1.0 + gate_pre * (1.0 - sigma))
    gate_dot = jnp.sum(hidden * grad_hidden, axis=1)
    scaled = gate * grad_hidden
    gated_hidden = (gate * hidden).astype(jnp.bfloat16)
    grad_gate_pre = (scaled * up_pre * slope).astype(jnp.bfloat16)
    grad_up_pre = (scaled * silu_value).astype(jnp.bfloat16)

    packed = jnp.concatenate([grad_gate_pre, grad_up_pre, gated_hidden], axis=1)
    far_packed = exchange(lambda j: packed, groups)

    part_out = dot(gated_hidden, down_mat, 1, 0).astype(jnp.bfloat16)
    output = lax.psum_scatter(part_out, PLANE, scatter_dimension=0, tiled=True)
    part_grad = (dot(grad_gate_pre, gate_mat, 1, 1) + dot(grad_up_pre, up_mat, 1, 1)).astype(
        jnp.bfloat16
    )
    grad_tokens = lax.psum_scatter(part_grad, PLANE, scatter_dimension=0, tiled=True)

    gate_dots = lax.all_gather(gate_dot, PLANE, axis=0, tiled=False)
    gate_dots = lax.dynamic_slice_in_dim(gate_dots, expert * local_tokens, local_tokens, 1)
    grad_gates = jnp.sum(jnp.where(chosen, gate_dots.T[:, None, :], 0.0), axis=2)

    ff = gate_mat.shape[1]
    rows = jnp.concatenate(
        [lax.dynamic_slice_in_dim(all_tokens, me * share, share, 1)]
        + [block[:, 0] for block in far],
        axis=0,
    )
    ups = jnp.concatenate(
        [lax.dynamic_slice_in_dim(all_upstream, me * share, share, 1)]
        + [block[:, 1] for block in far],
        axis=0,
    )
    every = jnp.concatenate([packed] + far_packed, axis=0)
    grad_w_gate = dot(rows, every[:, :ff], 0, 0).astype(jnp.bfloat16)[None]
    grad_w_up = dot(rows, every[:, ff : 2 * ff], 0, 0).astype(jnp.bfloat16)[None]
    grad_w_down = dot(every[:, 2 * ff :], ups, 0, 0).astype(jnp.bfloat16)[None]
    return (output, grad_tokens, grad_gates, grad_w_gate, grad_w_up, grad_w_down)


def solution(mesh):
    rows = P(("dp", "outer", "inner"), None)
    expert = P(("outer", "inner"), None, None)
    return jax.shard_map(
        local,
        mesh=mesh,
        in_specs=(rows, rows, rows, rows, expert, expert, expert),
        out_specs=(
            rows,
            rows,
            rows,
            P(("outer", "inner"), "dp", None),
            P(("outer", "inner"), "dp", None),
            P(("outer", "inner"), None, "dp"),
        ),
        check_vma=False,
    )
```

```python
import functools

import jax
import jax.numpy as jnp
from jax import lax
from jax.experimental import pallas as pl
from jax.experimental.pallas import tpu as pltpu
from jax.sharding import PartitionSpec as P

PLANE = ("outer", "inner")


def dot(left, right, left_dim, right_dim):
    return lax.dot_general(
        left,
        right,
        (((left_dim,), (right_dim,)), ((), ())),
        preferred_element_type=jnp.float32,
    )


MESH = pl.DeviceIdType.MESH
VMEM_LIMIT = 48 * 1024 * 1024


def place(sizes):
    highs, lows, _ = sizes
    outer = lax.axis_index("outer")
    return lax.axis_index("dp"), outer // lows, outer % lows, lax.axis_index("inner")


def greet(sizes):
    highs, lows, cores = sizes
    dp, hi, lo, core = place(sizes)
    peers = [(dp, (hi + d) % highs * lows + lo, core) for d in range(1, highs)]
    peers += [(dp, hi * lows + (lo + d) % lows, core) for d in range(1, lows)]
    peers += [(dp, hi * lows + lo, (core + d) % cores) for d in range(1, cores)]
    barrier = pltpu.get_barrier_semaphore()
    for peer in peers:
        pl.semaphore_signal(barrier, inc=1, device_id=peer, device_id_type=MESH)
    pl.semaphore_wait(barrier, len(peers))


def gather_kernel(sizes, chunks, *refs):
    highs, lows, cores = sizes
    count = len(refs) - 7
    sources, results = refs[: count // 2], refs[count // 2 : count]
    own_sem, hi_send, hi_recv, lo_send, lo_recv, core_send, core_recv = refs[count:]
    dp, hi, lo, core = place(sizes)
    mine = (hi * lows + lo) * cores + core
    greet(sizes)

    def block_of(high, low, at_core):
        return (high * lows + low) * cores + at_core

    def copy(src, dst, send, recv, outer, at_core):
        return pltpu.make_async_remote_copy(
            src_ref=src,
            dst_ref=dst,
            send_sem=send,
            recv_sem=recv,
            device_id=(dp, outer, at_core),
            device_id_type=MESH,
        )

    def to_hi(c, d):
        which, cols = chunks[c]
        return copy(
            sources[which].at[:, cols],
            results[which].at[mine, :, cols],
            hi_send.at[c, d],
            hi_recv.at[c, d],
            (hi + d) % highs * lows + lo,
            core,
        )

    def to_lo(c, d, h):
        which, cols = chunks[c]
        at = block_of((hi + highs - h) % highs, lo, core)
        src = sources[which].at[:, cols] if h == 0 else results[which].at[at, :, cols]
        return copy(
            src,
            results[which].at[at, :, cols],
            lo_send.at[c, d, h],
            lo_recv.at[c, d, h],
            hi * lows + (lo + d) % lows,
            core,
        )

    def to_core(c, d, h, e):
        which, cols = chunks[c]
        at = block_of((hi + highs - h) % highs, (lo + lows - d) % lows, core)
        src = sources[which].at[:, cols] if h == 0 and d == 0 else results[which].at[at, :, cols]
        return copy(
            src,
            results[which].at[at, :, cols],
            core_send.at[c, d, h, e],
            core_recv.at[c, d, h, e],
            hi * lows + lo,
            (core + e) % cores,
        )

    sent = []

    def start(what):
        what.start()
        sent.append(what)

    for c in range(len(chunks)):
        for d in range(1, lows):
            start(to_lo(c, d, 0))
        for d in range(1, highs):
            start(to_hi(c, d))
        for e in range(1, cores):
            start(to_core(c, 0, 0, e))
    kept = [
        pltpu.make_async_copy(sources[w], results[w].at[mine], own_sem.at[w])
        for w in range(count // 2)
    ]
    for one in kept:
        one.start()
    for c in range(len(chunks)):
        for h in range(1, highs):
            to_hi(c, h).wait_recv()
            for d in range(1, lows):
                start(to_lo(c, d, h))
            for e in range(1, cores):
                start(to_core(c, 0, h, e))
        for h in range(highs):
            for d in range(1, lows):
                to_lo(c, d, h).wait_recv()
                for e in range(1, cores):
                    start(to_core(c, d, h, e))
    for c in range(len(chunks)):
        for h in range(highs):
            for d in range(lows):
                for e in range(1, cores):
                    to_core(c, d, h, e).wait_recv()
    for one in kept:
        one.wait()
    for one in sent:
        one.wait_send()


def plane_sizes():
    outer = lax.axis_size("outer")
    highs = 4 if outer % 4 == 0 else 1
    return highs, outer // highs, lax.axis_size("inner")


def cut(arrays, width):
    chunks = []
    for which, value in enumerate(arrays):
        for first in range(0, value.shape[-1], width):
            chunks.append((which, pl.ds(first, min(width, value.shape[-1] - first))))
    return chunks


def gather_plane(arrays, width):
    sizes = highs, lows, cores = plane_sizes()
    blocks = highs * lows * cores
    chunks = cut(arrays, width)
    n = len(chunks)
    dma = pltpu.SemaphoreType.DMA
    got = pl.pallas_call(
        functools.partial(gather_kernel, sizes, chunks),
        out_shape=[jax.ShapeDtypeStruct((blocks,) + a.shape, a.dtype) for a in arrays],
        in_specs=[pl.BlockSpec(memory_space=pl.ANY)] * len(arrays),
        out_specs=[pl.BlockSpec(memory_space=pl.ANY)] * len(arrays),
        scratch_shapes=[
            dma((len(arrays),)),
            dma((n, highs)),
            dma((n, highs)),
            dma((n, lows, highs)),
            dma((n, lows, highs)),
            dma((n, lows, highs, cores)),
            dma((n, lows, highs, cores)),
        ],
        compiler_params=pltpu.CompilerParams(collective_id=0, has_side_effects=True),
        cost_estimate=pl.CostEstimate(flops=0, bytes_accessed=150_000_000, transcendentals=0),
    )(*arrays)
    return [g.reshape((-1,) + g.shape[2:]) for g in got]


def scatter_kernel(sizes, chunks, count, *refs):
    highs, lows, cores = sizes
    n = len(chunks)
    sources, results = refs[:count], refs[count : 2 * count]
    held, from_core, from_lo, half, from_hi = (
        refs[2 * count + n * k : 2 * count + n * (k + 1)] for k in range(5)
    )
    load_sem, core_send, core_recv, lo_send, lo_recv, hi_send, hi_recv = refs[2 * count + 5 * n :]
    dp, hi, lo, core = place(sizes)
    greet(sizes)

    def copy(src, dst, send, recv, outer, at_core):
        return pltpu.make_async_remote_copy(
            src_ref=src,
            dst_ref=dst,
            send_sem=send,
            recv_sem=recv,
            device_id=(dp, outer, at_core),
            device_id_type=MESH,
        )

    def load(c):
        which, cols = chunks[c]
        return pltpu.make_async_copy(
            sources[which].at[:, :, core, :, cols], held[c], load_sem.at[c]
        )

    def to_core(c, e):
        which, cols = chunks[c]
        return copy(
            sources[which].at[:, :, (core + e) % cores, :, cols],
            from_core[c].at[e - 1],
            core_send.at[c, e],
            core_recv.at[c, e],
            hi * lows + lo,
            (core + e) % cores,
        )

    def to_lo(c, d):
        return copy(
            held[c].at[:, (lo + d) % lows],
            from_lo[c].at[d - 1],
            lo_send.at[c, d],
            lo_recv.at[c, d],
            hi * lows + (lo + d) % lows,
            core,
        )

    def to_hi(c, d):
        return copy(
            half[c].at[(hi + d) % highs],
            from_hi[c].at[d - 1],
            hi_send.at[c, d],
            hi_recv.at[c, d],
            (hi + d) % highs * lows + lo,
            core,
        )

    def over_cores(c):
        load(c).wait()
        for e in range(1, cores):
            to_core(c, e).wait_recv()
        for h in range(highs):
            for l in range(lows):
                total = held[c][h, l].astype(jnp.float32)
                for e in range(1, cores):
                    total += from_core[c][e - 1, h, l].astype(jnp.float32)
                held[c][h, l] = total.astype(held[c].dtype)
        for d in range(1, lows):
            to_lo(c, d).start()

    def over_lo(c):
        for d in range(1, lows):
            to_lo(c, d).wait_recv()
        for h in range(highs):
            total = held[c][h, lo].astype(jnp.float32)
            for d in range(1, lows):
                total += from_lo[c][d - 1, h].astype(jnp.float32)
            half[c][h] = total.astype(half[c].dtype)
        for d in range(1, highs):
            to_hi(c, d).start()

    def over_hi(c):
        which, cols = chunks[c]
        for d in range(1, highs):
            to_hi(c, d).wait_recv()
        total = half[c][hi].astype(jnp.float32)
        for d in range(1, highs):
            total += from_hi[c][d - 1].astype(jnp.float32)
        results[which][:, cols] = total.astype(results[which].dtype)

    for c in range(n):
        for e in range(1, cores):
            to_core(c, e).start()
        load(c).start()
    for step in range(n + 4):
        if step < n:
            over_cores(step)
        if 0 <= step - 2 < n:
            over_lo(step - 2)
        if 0 <= step - 4:
            over_hi(step - 4)
    for c in range(n):
        for e in range(1, cores):
            to_core(c, e).wait_send()
        for d in range(1, lows):
            to_lo(c, d).wait_send()
        for d in range(1, highs):
            to_hi(c, d).wait_send()


def scatter_plane(arrays, width):
    sizes = highs, lows, cores = plane_sizes()
    rows = arrays[0].shape[0] // (highs * lows * cores)
    arrays = [a.reshape(highs, lows, cores, rows, a.shape[-1]) for a in arrays]
    chunks = cut(arrays, width)
    n = len(chunks)
    dma = pltpu.SemaphoreType.DMA
    kinds = [(arrays[which].dtype, cols.size) for which, cols in chunks]

    def buffers(*lead):
        return [pltpu.VMEM(lead + (rows, w), t) for t, w in kinds]

    return pl.pallas_call(
        functools.partial(scatter_kernel, sizes, chunks, len(arrays)),
        out_shape=[jax.ShapeDtypeStruct((rows, a.shape[-1]), a.dtype) for a in arrays],
        in_specs=[pl.BlockSpec(memory_space=pl.ANY)] * len(arrays),
        out_specs=[pl.BlockSpec(memory_space=pltpu.VMEM)] * len(arrays),
        scratch_shapes=[
            *buffers(highs, lows),
            *buffers(max(cores - 1, 1), highs, lows),
            *buffers(max(lows - 1, 1), highs),
            *buffers(highs),
            *buffers(max(highs - 1, 1)),
            dma((n,)),
            dma((n, cores)),
            dma((n, cores)),
            dma((n, lows)),
            dma((n, lows)),
            dma((n, highs)),
            dma((n, highs)),
        ],
        compiler_params=pltpu.CompilerParams(
            collective_id=1, has_side_effects=True, vmem_limit_bytes=VMEM_LIMIT
        ),
        cost_estimate=pl.CostEstimate(flops=0, bytes_accessed=180_000_000, transcendentals=0),
    )(*arrays)


def exchange(block_for, count):
    me = lax.axis_index("dp")
    got = []
    for shift in range(1, count):
        pairs = [(q, (q + shift) % count) for q in range(count)]
        got.append(lax.ppermute(block_for((me + shift) % count), "dp", pairs))
    return got


def local(tokens, expert_ids, gate_values, upstream, w_gate, w_up, w_down):
    local_tokens, width = tokens.shape
    groups = lax.axis_size("dp")
    inner_count = lax.axis_size("inner")
    expert_count = lax.axis_size("outer") * inner_count
    me = lax.axis_index("dp")
    expert = lax.axis_index("outer") * inner_count + lax.axis_index("inner")
    share = width // groups
    gate_mat, up_mat, down_mat = w_gate[0], w_up[0], w_down[0]

    def plane_gather(value):
        return lax.all_gather(value, PLANE, axis=0, tiled=True)

    chosen = expert_ids[:, :, None] == jnp.arange(expert_count, dtype=jnp.int32)[None, None, :]
    gate_grid = jnp.sum(jnp.where(chosen, gate_values[:, :, None], 0.0), axis=1)

    lanes = jnp.pad(gate_grid, ((0, 0), (0, -expert_count % 128)))
    all_gates, all_tokens, all_upstream = gather_plane([lanes, tokens, upstream], 2048)
    all_gates = all_gates[:, :expert_count]
    both = jnp.stack([tokens, upstream], axis=1)
    far = exchange(lambda j: lax.dynamic_slice_in_dim(both, j * share, share, 2), groups)
    *far, all_gates = lax.optimization_barrier((*far, all_gates))
    far = [plane_gather(block) for block in far]

    is_mine = jnp.arange(expert_count, dtype=jnp.int32) == expert
    gate = jnp.sum(jnp.where(is_mine[None, :], all_gates, 0.0), axis=1, keepdims=True)

    gate_pre = dot(all_tokens, gate_mat, 1, 0)
    up_pre = dot(all_tokens, up_mat, 1, 0)
    grad_hidden = dot(all_upstream, down_mat, 1, 1)
    sigma = jax.nn.sigmoid(gate_pre)
    silu_value = gate_pre * sigma
    hidden = silu_value * up_pre
    slope = sigma * (1.0 + gate_pre * (1.0 - sigma))
    gate_dot = jnp.sum(hidden * grad_hidden, axis=1)
    scaled = gate * grad_hidden
    gated_hidden = (gate * hidden).astype(jnp.bfloat16)
    grad_gate_pre = (scaled * up_pre * slope).astype(jnp.bfloat16)
    grad_up_pre = (scaled * silu_value).astype(jnp.bfloat16)

    packed = jnp.concatenate([grad_gate_pre, grad_up_pre, gated_hidden], axis=1)
    far_packed = exchange(lambda j: packed, groups)

    part_out = dot(gated_hidden, down_mat, 1, 0).astype(jnp.bfloat16)
    part_grad = (dot(grad_gate_pre, gate_mat, 1, 1) + dot(grad_up_pre, up_mat, 1, 1)).astype(
        jnp.bfloat16
    )
    lane = jnp.arange(lanes.shape[1], dtype=jnp.int32)
    dots = jnp.where(lane[None, :] == expert, gate_dot[:, None], 0.0)
    dots, output, grad_tokens = scatter_plane([dots, part_out, part_grad], 1024)
    grad_gates = jnp.sum(jnp.where(chosen, dots[:, None, :expert_count], 0.0), axis=2)

    ff = gate_mat.shape[1]
    rows = jnp.concatenate(
        [lax.dynamic_slice_in_dim(all_tokens, me * share, share, 1)]
        + [block[:, 0] for block in far],
        axis=0,
    )
    ups = jnp.concatenate(
        [lax.dynamic_slice_in_dim(all_upstream, me * share, share, 1)]
        + [block[:, 1] for block in far],
        axis=0,
    )
    every = jnp.concatenate([packed] + far_packed, axis=0)
    grad_w_gate = dot(rows, every[:, :ff], 0, 0).astype(jnp.bfloat16)[None]
    grad_w_up = dot(rows, every[:, ff : 2 * ff], 0, 0).astype(jnp.bfloat16)[None]
    grad_w_down = dot(every[:, 2 * ff :], ups, 0, 0).astype(jnp.bfloat16)[None]
    return (output, grad_tokens, grad_gates, grad_w_gate, grad_w_up, grad_w_down)


def solution(mesh):
    rows = P(("dp", "outer", "inner"), None)
    expert = P(("outer", "inner"), None, None)
    return jax.shard_map(
        local,
        mesh=mesh,
        in_specs=(rows, rows, rows, rows, expert, expert, expert),
        out_specs=(
            rows,
            rows,
            rows,
            P(("outer", "inner"), "dp", None),
            P(("outer", "inner"), "dp", None),
            P(("outer", "inner"), None, "dp"),
        ),
        check_vma=False,
    )
```

```python
import functools

import jax
import jax.numpy as jnp
from jax import lax
from jax.experimental import pallas as pl
from jax.experimental.pallas import tpu as pltpu
from jax.sharding import PartitionSpec as P

PLANE = ("outer", "inner")


def dot(left, right, left_dim, right_dim):
    return lax.dot_general(
        left,
        right,
        (((left_dim,), (right_dim,)), ((), ())),
        preferred_element_type=jnp.float32,
    )


MESH = pl.DeviceIdType.MESH
VMEM_LIMIT = 48 * 1024 * 1024


def place(sizes):
    highs, lows, _ = sizes
    outer = lax.axis_index("outer")
    return lax.axis_index("dp"), outer // lows, outer % lows, lax.axis_index("inner")


def greet(sizes, groups):
    highs, lows, cores = sizes
    dp, hi, lo, core = place(sizes)
    peers = [(dp, (hi + d) % highs * lows + lo, core) for d in range(1, highs)]
    peers += [(dp, hi * lows + (lo + d) % lows, core) for d in range(1, lows)]
    peers += [(dp, hi * lows + lo, (core + d) % cores) for d in range(1, cores)]
    peers += [((dp + d) % groups, hi * lows + lo, core) for d in range(1, groups)]
    barrier = pltpu.get_barrier_semaphore()
    for peer in peers:
        pl.semaphore_signal(barrier, inc=1, device_id=peer, device_id_type=MESH)
    pl.semaphore_wait(barrier, len(peers))


def gather_kernel(sizes, groups, chunks, count, *refs):
    highs, lows, cores = sizes
    sources, results = refs[:count], refs[count : 2 * count]
    fars = refs[2 * count : -9]
    own_sem, hi_send, hi_recv, lo_send, lo_recv, core_send, core_recv, far_send, far_recv = refs[-9:]
    dp, hi, lo, core = place(sizes)
    mine = (hi * lows + lo) * cores + core
    greet(sizes, groups)

    def block_of(high, low, at_core):
        return (high * lows + low) * cores + at_core

    def copy(src, dst, send, recv, outer, at_core):
        return pltpu.make_async_remote_copy(
            src_ref=src,
            dst_ref=dst,
            send_sem=send,
            recv_sem=recv,
            device_id=(dp, outer, at_core),
            device_id_type=MESH,
        )

    def to_hi(c, d):
        which, cols = chunks[c]
        return copy(
            sources[which].at[:, cols],
            results[which].at[mine, :, cols],
            hi_send.at[c, d],
            hi_recv.at[c, d],
            (hi + d) % highs * lows + lo,
            core,
        )

    def to_lo(c, d, h):
        which, cols = chunks[c]
        at = block_of((hi + highs - h) % highs, lo, core)
        src = sources[which].at[:, cols] if h == 0 else results[which].at[at, :, cols]
        return copy(
            src,
            results[which].at[at, :, cols],
            lo_send.at[c, d, h],
            lo_recv.at[c, d, h],
            hi * lows + (lo + d) % lows,
            core,
        )

    def to_core(c, d, h, e):
        which, cols = chunks[c]
        at = block_of((hi + highs - h) % highs, (lo + lows - d) % lows, core)
        src = sources[which].at[:, cols] if h == 0 and d == 0 else results[which].at[at, :, cols]
        return copy(
            src,
            results[which].at[at, :, cols],
            core_send.at[c, d, h, e],
            core_recv.at[c, d, h, e],
            hi * lows + lo,
            (core + e) % cores,
        )

    def to_group(k, s):
        src = sources[count - len(fars) + k]
        share = src.shape[1] // groups
        group = (dp + s) % groups
        return pltpu.make_async_remote_copy(
            src_ref=src.at[:, pl.ds(pl.multiple_of(group * share, share), share)],
            dst_ref=fars[k].at[s - 1],
            send_sem=far_send.at[k, s],
            recv_sem=far_recv.at[k, s],
            device_id=(group, hi * lows + lo, core),
            device_id_type=MESH,
        )

    sent = []

    def start(what):
        what.start()
        sent.append(what)

    for k in range(len(fars)):
        for s in range(1, groups):
            start(to_group(k, s))
    for c in range(len(chunks)):
        for d in range(1, lows):
            start(to_lo(c, d, 0))
        for d in range(1, highs):
            start(to_hi(c, d))
        for e in range(1, cores):
            start(to_core(c, 0, 0, e))
    kept = [
        pltpu.make_async_copy(sources[w], results[w].at[mine], own_sem.at[w])
        for w in range(count)
    ]
    for one in kept:
        one.start()
    for c in range(len(chunks)):
        for h in range(1, highs):
            to_hi(c, h).wait_recv()
            for d in range(1, lows):
                start(to_lo(c, d, h))
            for e in range(1, cores):
                start(to_core(c, 0, h, e))
        for h in range(highs):
            for d in range(1, lows):
                to_lo(c, d, h).wait_recv()
                for e in range(1, cores):
                    start(to_core(c, d, h, e))
    for c in range(len(chunks)):
        for h in range(highs):
            for d in range(lows):
                for e in range(1, cores):
                    to_core(c, d, h, e).wait_recv()
    for k in range(len(fars)):
        for s in range(1, groups):
            to_group(k, s).wait_recv()
    for one in kept:
        one.wait()
    for one in sent:
        one.wait_send()


def plane_sizes():
    outer = lax.axis_size("outer")
    highs = 4 if outer % 4 == 0 else 1
    return highs, outer // highs, lax.axis_size("inner")


def cut(arrays, width):
    chunks = []
    for which, value in enumerate(arrays):
        for first in range(0, value.shape[-1], width):
            chunks.append((which, pl.ds(first, min(width, value.shape[-1] - first))))
    return chunks


def gather_plane(arrays, far_count, width):
    groups = lax.axis_size("dp")
    others = arrays[len(arrays) - far_count :] if groups > 1 else []
    sizes = highs, lows, cores = plane_sizes()
    blocks = highs * lows * cores
    chunks = cut(arrays, width)
    n = len(chunks)
    dma = pltpu.SemaphoreType.DMA
    got = pl.pallas_call(
        functools.partial(gather_kernel, sizes, groups, chunks, len(arrays)),
        out_shape=[jax.ShapeDtypeStruct((blocks,) + a.shape, a.dtype) for a in arrays]
        + [
            jax.ShapeDtypeStruct((groups - 1, a.shape[0], a.shape[1] // groups), a.dtype)
            for a in others
        ],
        in_specs=[pl.BlockSpec(memory_space=pl.ANY)] * len(arrays),
        out_specs=[pl.BlockSpec(memory_space=pl.ANY)] * (len(arrays) + len(others)),
        scratch_shapes=[
            dma((len(arrays),)),
            dma((n, highs)),
            dma((n, highs)),
            dma((n, lows, highs)),
            dma((n, lows, highs)),
            dma((n, lows, highs, cores)),
            dma((n, lows, highs, cores)),
            dma((far_count, groups)),
            dma((far_count, groups)),
        ],
        compiler_params=pltpu.CompilerParams(collective_id=0, has_side_effects=True),
        cost_estimate=pl.CostEstimate(flops=0, bytes_accessed=150_000_000, transcendentals=0),
    )(*arrays)
    whole = [g.reshape((-1,) + g.shape[2:]) for g in got[: len(arrays)]]
    return whole, got[len(arrays) :]


def scatter_kernel(sizes, chunks, count, *refs):
    highs, lows, cores = sizes
    n = len(chunks)
    sources, results = refs[:count], refs[count : 2 * count]
    held, from_core, from_lo, half, from_hi = (
        refs[2 * count + n * k : 2 * count + n * (k + 1)] for k in range(5)
    )
    load_sem, core_send, core_recv, lo_send, lo_recv, hi_send, hi_recv = refs[2 * count + 5 * n :]
    dp, hi, lo, core = place(sizes)
    greet(sizes, 1)

    def copy(src, dst, send, recv, outer, at_core):
        return pltpu.make_async_remote_copy(
            src_ref=src,
            dst_ref=dst,
            send_sem=send,
            recv_sem=recv,
            device_id=(dp, outer, at_core),
            device_id_type=MESH,
        )

    def load(c):
        which, cols = chunks[c]
        return pltpu.make_async_copy(
            sources[which].at[:, :, core, :, cols], held[c], load_sem.at[c]
        )

    def to_core(c, e):
        which, cols = chunks[c]
        return copy(
            sources[which].at[:, :, (core + e) % cores, :, cols],
            from_core[c].at[e - 1],
            core_send.at[c, e],
            core_recv.at[c, e],
            hi * lows + lo,
            (core + e) % cores,
        )

    def to_lo(c, d):
        return copy(
            held[c].at[:, (lo + d) % lows],
            from_lo[c].at[d - 1],
            lo_send.at[c, d],
            lo_recv.at[c, d],
            hi * lows + (lo + d) % lows,
            core,
        )

    def to_hi(c, d):
        return copy(
            half[c].at[(hi + d) % highs],
            from_hi[c].at[d - 1],
            hi_send.at[c, d],
            hi_recv.at[c, d],
            (hi + d) % highs * lows + lo,
            core,
        )

    def over_cores(c):
        load(c).wait()
        for e in range(1, cores):
            to_core(c, e).wait_recv()
        for h in range(highs):
            for l in range(lows):
                total = held[c][h, l].astype(jnp.float32)
                for e in range(1, cores):
                    total += from_core[c][e - 1, h, l].astype(jnp.float32)
                held[c][h, l] = total.astype(held[c].dtype)
        for d in range(1, lows):
            to_lo(c, d).start()

    def over_lo(c):
        for d in range(1, lows):
            to_lo(c, d).wait_recv()
        for h in range(highs):
            total = held[c][h, lo].astype(jnp.float32)
            for d in range(1, lows):
                total += from_lo[c][d - 1, h].astype(jnp.float32)
            half[c][h] = total.astype(half[c].dtype)
        for d in range(1, highs):
            to_hi(c, d).start()

    def over_hi(c):
        which, cols = chunks[c]
        for d in range(1, highs):
            to_hi(c, d).wait_recv()
        total = half[c][hi].astype(jnp.float32)
        for d in range(1, highs):
            total += from_hi[c][d - 1].astype(jnp.float32)
        results[which][:, cols] = total.astype(results[which].dtype)

    for c in range(n):
        for e in range(1, cores):
            to_core(c, e).start()
        load(c).start()
    for step in range(n + 4):
        if step < n:
            over_cores(step)
        if 0 <= step - 2 < n:
            over_lo(step - 2)
        if 0 <= step - 4:
            over_hi(step - 4)
    for c in range(n):
        for e in range(1, cores):
            to_core(c, e).wait_send()
        for d in range(1, lows):
            to_lo(c, d).wait_send()
        for d in range(1, highs):
            to_hi(c, d).wait_send()


def scatter_plane(arrays, width):
    sizes = highs, lows, cores = plane_sizes()
    rows = arrays[0].shape[0] // (highs * lows * cores)
    arrays = [a.reshape(highs, lows, cores, rows, a.shape[-1]) for a in arrays]
    chunks = cut(arrays, width)
    n = len(chunks)
    dma = pltpu.SemaphoreType.DMA
    kinds = [(arrays[which].dtype, cols.size) for which, cols in chunks]

    def buffers(*lead):
        return [pltpu.VMEM(lead + (rows, w), t) for t, w in kinds]

    return pl.pallas_call(
        functools.partial(scatter_kernel, sizes, chunks, len(arrays)),
        out_shape=[jax.ShapeDtypeStruct((rows, a.shape[-1]), a.dtype) for a in arrays],
        in_specs=[pl.BlockSpec(memory_space=pl.ANY)] * len(arrays),
        out_specs=[pl.BlockSpec(memory_space=pltpu.VMEM)] * len(arrays),
        scratch_shapes=[
            *buffers(highs, lows),
            *buffers(max(cores - 1, 1), highs, lows),
            *buffers(max(lows - 1, 1), highs),
            *buffers(highs),
            *buffers(max(highs - 1, 1)),
            dma((n,)),
            dma((n, cores)),
            dma((n, cores)),
            dma((n, lows)),
            dma((n, lows)),
            dma((n, highs)),
            dma((n, highs)),
        ],
        compiler_params=pltpu.CompilerParams(
            collective_id=1, has_side_effects=True, vmem_limit_bytes=VMEM_LIMIT
        ),
        cost_estimate=pl.CostEstimate(flops=0, bytes_accessed=180_000_000, transcendentals=0),
    )(*arrays)


def exchange(block_for, count):
    me = lax.axis_index("dp")
    got = []
    for shift in range(1, count):
        pairs = [(q, (q + shift) % count) for q in range(count)]
        got.append(lax.ppermute(block_for((me + shift) % count), "dp", pairs))
    return got


def local(tokens, expert_ids, gate_values, upstream, w_gate, w_up, w_down):
    local_tokens, width = tokens.shape
    groups = lax.axis_size("dp")
    inner_count = lax.axis_size("inner")
    expert_count = lax.axis_size("outer") * inner_count
    me = lax.axis_index("dp")
    expert = lax.axis_index("outer") * inner_count + lax.axis_index("inner")
    share = width // groups
    gate_mat, up_mat, down_mat = w_gate[0], w_up[0], w_down[0]

    def plane_gather(value):
        return lax.all_gather(value, PLANE, axis=0, tiled=True)

    chosen = expert_ids[:, :, None] == jnp.arange(expert_count, dtype=jnp.int32)[None, None, :]
    gate_grid = jnp.sum(jnp.where(chosen, gate_values[:, :, None], 0.0), axis=1)

    lanes = jnp.pad(gate_grid, ((0, 0), (0, -expert_count % 128)))
    (all_gates, all_tokens, all_upstream), far = gather_plane([lanes, tokens, upstream], 2, 2048)
    all_gates = all_gates[:, :expert_count]
    far = [[plane_gather(blocks[s]) for s in range(groups - 1)] for blocks in far]

    is_mine = jnp.arange(expert_count, dtype=jnp.int32) == expert
    gate = jnp.sum(jnp.where(is_mine[None, :], all_gates, 0.0), axis=1, keepdims=True)

    gate_pre = dot(all_tokens, gate_mat, 1, 0)
    up_pre = dot(all_tokens, up_mat, 1, 0)
    grad_hidden = dot(all_upstream, down_mat, 1, 1)
    sigma = jax.nn.sigmoid(gate_pre)
    silu_value = gate_pre * sigma
    hidden = silu_value * up_pre
    slope = sigma * (1.0 + gate_pre * (1.0 - sigma))
    gate_dot = jnp.sum(hidden * grad_hidden, axis=1)
    scaled = gate * grad_hidden
    gated_hidden = (gate * hidden).astype(jnp.bfloat16)
    grad_gate_pre = (scaled * up_pre * slope).astype(jnp.bfloat16)
    grad_up_pre = (scaled * silu_value).astype(jnp.bfloat16)

    packed = jnp.concatenate([grad_gate_pre, grad_up_pre, gated_hidden], axis=1)
    far_packed = exchange(lambda j: packed, groups)

    part_out = dot(gated_hidden, down_mat, 1, 0).astype(jnp.bfloat16)
    part_grad = (dot(grad_gate_pre, gate_mat, 1, 1) + dot(grad_up_pre, up_mat, 1, 1)).astype(
        jnp.bfloat16
    )
    lane = jnp.arange(lanes.shape[1], dtype=jnp.int32)
    dots = jnp.where(lane[None, :] == expert, gate_dot[:, None], 0.0)
    dots, output, grad_tokens = scatter_plane([dots, part_out, part_grad], 1024)
    grad_gates = jnp.sum(jnp.where(chosen, dots[:, None, :expert_count], 0.0), axis=2)

    ff = gate_mat.shape[1]
    rows = [lax.dynamic_slice_in_dim(all_tokens, me * share, share, 1), *far[0]]
    ups = [lax.dynamic_slice_in_dim(all_upstream, me * share, share, 1), *far[1]]
    every = [packed, *far_packed]

    def summed(lefts, rights):
        total = dot(lefts[0], rights[0], 0, 0)
        for left, right in zip(lefts[1:], rights[1:]):
            total += dot(left, right, 0, 0)
        return total.astype(jnp.bfloat16)[None]

    grad_w_gate = summed(rows, [each[:, :ff] for each in every])
    grad_w_up = summed(rows, [each[:, ff : 2 * ff] for each in every])
    grad_w_down = summed([each[:, 2 * ff :] for each in every], ups)
    return (output, grad_tokens, grad_gates, grad_w_gate, grad_w_up, grad_w_down)


def solution(mesh):
    rows = P(("dp", "outer", "inner"), None)
    expert = P(("outer", "inner"), None, None)
    return jax.shard_map(
        local,
        mesh=mesh,
        in_specs=(rows, rows, rows, rows, expert, expert, expert),
        out_specs=(
            rows,
            rows,
            rows,
            P(("outer", "inner"), "dp", None),
            P(("outer", "inner"), "dp", None),
            P(("outer", "inner"), None, "dp"),
        ),
        check_vma=False,
    )
```
